512 devices in a mesh: corpus: 64 (over y, x, core), tile: 8 (over z).
Axes of the slice: x: 4, y: 8, z: 8, core: 2. Of those that a mesh axis runs over, the one named last changes fastest.
Arguments:
- embeddings: bfloat16 [131072, 1024], P('corpus'), may hold values from -250 to 250
- cluster_ids: int32 [131072], P('corpus'), may hold values from 0 to 63, as said below
Outputs:
- best_match: float32 [131072], P('corpus')
The draws below stay inside these ranges and needn't reach their ends.
Inputs may be any that keep to these rules, and one draw needn't show every extreme that they name: `cluster_ids`: within each aligned block of 2048 rows (the rows of one index of corpus) no cluster appears more than 64 times, and one cluster appears exactly 64 times in every block.
All inputs are finite; a program needn't handle non-finite values.
Results may differ from the reference program's by a relative error of at most 0.00055.
Values may be sent and summed in bfloat16 or wider, within the bound.
A program may use at most 64 MiB of HBM per device.

```python
import math
import jax
import jax.numpy as jnp
from jax import lax

D = 1024
ROWS_DEV = 2048
CLUSTERS = 64
M = 64
ROWS = 131072


def draw_ids(key):
    key = jax.random.fold_in(key, 101)
    heat_key, forced_key, block_key = jax.random.split(key, 3)
    heat = jax.random.randint(heat_key, (CLUSTERS,), 0, 4)
    forced = jax.random.randint(forced_key, (), 0, CLUSTERS)
    pool = jnp.arange(CLUSTERS * M) // M

    def one_block(bkey):
        score_key, order_key = jax.random.split(bkey)
        base = jax.random.randint(score_key, (CLUSTERS * M,), 0, 2 ** 14)
        score = base + heat[pool] * 2 ** 13 + jnp.where(pool == forced, 2 ** 16, 0)
        distinct = score * 4096 + jnp.arange(CLUSTERS * M)
        picked = jax.lax.top_k(distinct, ROWS_DEV)[1]
        chosen = pool[picked]
        return chosen[jax.random.permutation(order_key, ROWS_DEV)]
    blocks = jax.vmap(one_block)(jax.random.split(block_key, CLUSTERS))
    return blocks.reshape(ROWS).astype(jnp.int32)


def draw_cluster_ids(key, part):
    return draw_ids(key)


def draw_embeddings(key, part):
    ids = draw_ids(key)
    key = jax.random.fold_in(key, 7)
    center_key, noise_key, pull_key, scale_key = jax.random.split(key, 4)
    centers = jax.random.normal(center_key, (CLUSTERS, D), jnp.float32)
    noise = jax.random.normal(noise_key, (ROWS, D), jnp.float32)
    pull = jax.random.uniform(pull_key, (ROWS, 1), jnp.float32, 0.2, 1.2)
    scale = jnp.exp(jax.random.uniform(scale_key, (ROWS, 1), jnp.float32, 0.0, math.log(10.0)))
    values = scale * (pull * centers[ids] + noise)
    return jnp.clip(values, -250.0, 250.0).astype(jnp.bfloat16)


def setup_inputs(seed: int = 0) -> dict:
    key_list = jax.random.split(jax.random.key(seed), 3)
    embeddings = draw_embeddings(jax.random.fold_in(key_list[2], 71), 0)
    cluster_ids = draw_cluster_ids(jax.random.fold_in(key_list[2], 71), 0)
    return dict(embeddings=embeddings, cluster_ids=cluster_ids)


EPS = 1e-06

def unit_rows(embeddings):
    values = embeddings.astype(jnp.float32)
    total = lax.optimization_barrier(jnp.sum(values * values, axis=-1, keepdims=True))
    return (values * lax.rsqrt(total + EPS)).astype(jnp.bfloat16)

def reference(embeddings, cluster_ids):
    unit = unit_rows(embeddings)
    capacity = CLUSTERS * M

    def one_cluster(which):
        members = jnp.nonzero(cluster_ids == which, size=capacity, fill_value=ROWS)[0].astype(jnp.int32)
        present = members < ROWS
        picked = jnp.take(unit, jnp.minimum(members, ROWS - 1), axis=0).astype(jnp.float32)
        scores = jnp.dot(picked, picked.T, precision=lax.Precision.HIGHEST, preferred_element_type=jnp.float32)
        other = jnp.arange(capacity)[:, None] != jnp.arange(capacity)[None, :]
        keep = present[None, :] & other
        best = lax.optimization_barrier(jnp.max(jnp.where(keep, scores, jnp.float32(-1.0)), axis=1))
        return (members, best)
    members, best = lax.map(one_cluster, jnp.arange(CLUSTERS).astype(jnp.int32))
    result = jnp.full((ROWS,), -1.0, jnp.float32)
    return result.at[members.reshape(-1)].set(best.reshape(-1), mode='drop')
```

```python
import functools

import jax
import jax.numpy as jnp
from jax import lax
from jax.experimental import pallas as pl
from jax.experimental.pallas import tpu as pltpu
from jax.sharding import PartitionSpec as P

EPS = 1e-06
MESH = pl.DeviceIdType.MESH
NY, NX, NZ = 8, 4, 8
SLOTS = 64
PIECES = 4
PIECE_RANKS = SLOTS // PIECES
PIECE = NY * PIECE_RANKS
UNIT = NY * SLOTS
LANES = 128
MARK = 4.0
NEG = -1e6


def corpus_id(y, x, k):
    return (y * NX + x) * 2 + k


def inner(left, right):
    return lax.dot_general(
        left, right, (((1,), (1,)), ((), ())), preferred_element_type=jnp.float32
    )


def row_bias(unit):
    head = unit[:, :LANES].astype(jnp.float32)
    return jnp.where(head > MARK / 2, jnp.float32(NEG), jnp.float32(0.0))


def lane_bias(unit):
    first = (lax.broadcasted_iota(jnp.int32, (16, LANES), 1) == 0).astype(jnp.bfloat16)
    head = inner(first, unit[:, :LANES])[0:1]
    return jnp.where(head > MARK / 2, jnp.float32(NEG), jnp.float32(0.0))


def kernel(
    emb_hbm, ids_ref, out_ref,
    emb, outbox, obuf, lbuf, rbuf, part_out, part_in, ret_y, ret_z,
    emb_sem, own_sem, ysend, yrecv, fsend, frecv, psend, precv, ry_send, ry_recv, rz_send, rz_recv,
):
    corpus = lax.axis_index("corpus")
    z = lax.axis_index("tile")
    y, x, k = corpus // (NX * 2), (corpus // 2) % NX, corpus % 2
    right, left = (x + 1) % NX, (x + NX - 1) % NX
    right_core = (k + x // 2) % 2
    left_core = (k + left // 2) % 2
    sib = corpus_id(y, x, 1 - k)

    load = pltpu.make_async_copy(emb_hbm, emb, emb_sem)
    load.start()

    barrier = pltpu.get_barrier_semaphore()

    def greet(corpus_to, tile_to):
        pl.semaphore_signal(barrier, inc=1, device_id=(corpus_to, tile_to), device_id_type=MESH)

    for d in range(1, NY):
        greet(corpus_id((y + d) % NY, x, k), z)
    for d in range(1, NZ):
        greet(corpus, (z + d) % NZ)
    for core in range(2):
        greet(corpus_id(y, right, core), z)
        greet(corpus_id(y, left, core), z)
    greet(sib, z)

    ids = ids_ref[...]
    rows = ids.shape[1]
    clusters = NY * NZ
    member = lax.broadcasted_iota(jnp.int32, (clusters, rows), 0) == ids
    onehot = jnp.where(member, jnp.float32(1.0), jnp.float32(0.0)).astype(jnp.bfloat16)
    step = 256
    row_i = lax.broadcasted_iota(jnp.int32, (step, step + LANES), 0)
    col_i = lax.broadcasted_iota(jnp.int32, (step, step + LANES), 1)
    earlier = ((row_i < col_i) | (col_i >= step)).astype(jnp.bfloat16)
    carry = jnp.zeros((clusters, LANES), jnp.float32)
    ranks = []
    for b in range(rows // step):
        part = onehot[:, b * step:(b + 1) * step]
        count = jnp.dot(part, earlier, preferred_element_type=jnp.float32)
        before = count[:, :step] + jnp.concatenate([carry] * (step // LANES), axis=1)
        ranks.append(jnp.sum(before * part.astype(jnp.float32), axis=0, keepdims=True))
        carry = carry + count[:, step:]
    rank = jnp.concatenate(ranks, axis=1)
    key = (ids - z * NY) * SLOTS + rank.astype(jnp.int32)

    load.wait()

    def y_copy(d, p):
        to = (y + d) % NY
        return pltpu.make_async_remote_copy(
            src_ref=outbox.at[p, to],
            dst_ref=obuf.at[0, pl.ds(pl.multiple_of(p * PIECE + y * PIECE_RANKS, 16), PIECE_RANKS)],
            send_sem=ysend.at[p, d],
            recv_sem=yrecv.at[p, d],
            device_id=(corpus_id(to, x, k), z),
            device_id_type=MESH,
        )

    def y_arrival(d, p):
        source = (y + NY - d) % NY
        return pltpu.make_async_remote_copy(
            src_ref=outbox.at[p, source],
            dst_ref=obuf.at[0, pl.ds(pl.multiple_of(p * PIECE + source * PIECE_RANKS, 16), PIECE_RANKS)],
            send_sem=ysend.at[p, d],
            recv_sem=yrecv.at[p, d],
            device_id=(corpus_id(source, x, k), z),
            device_id_type=MESH,
        )

    def own_copy(p):
        return pltpu.make_async_copy(
            outbox.at[p, y],
            obuf.at[0, pl.ds(pl.multiple_of(p * PIECE + y * PIECE_RANKS, 16), PIECE_RANKS)],
            own_sem.at[p],
        )

    order = (4, 3, 5, 2, 6, 1, 7)
    slot_i = lax.broadcasted_iota(jnp.int32, (PIECE, 1), 0)
    lane_i = lax.broadcasted_iota(jnp.int32, (PIECE, emb.shape[1]), 1)
    for p in range(PIECES):
        wanted = (slot_i // PIECE_RANKS) * SLOTS + p * PIECE_RANKS + slot_i % PIECE_RANKS
        pick = jnp.where(wanted == key, jnp.float32(1.0), jnp.float32(0.0))
        filled = jnp.sum(pick, axis=1, keepdims=True)
        values = jnp.dot(pick.astype(jnp.bfloat16), emb[...], preferred_element_type=jnp.float32)
        total = jnp.sum(values * values, axis=1, keepdims=True)
        empty = jnp.where(lane_i < LANES, jnp.float32(MARK), jnp.float32(0.0))
        unit = jnp.where(filled > 0.5, values * lax.rsqrt(total + EPS), empty)
        outbox[p] = unit.astype(jnp.bfloat16).reshape(NY, PIECE_RANKS, emb.shape[1])
        if p == 0:
            pl.semaphore_wait(barrier, NY - 1 + NZ - 1 + 5)
        for d in order:
            y_copy(d, p).start()
        own_copy(p).start()

    def forward(p, way):
        there = pl.ds(p * PIECE, PIECE)
        target, to = (
            (lbuf.at[there], corpus_id(y, right, k)),
            (rbuf.at[there], corpus_id(y, left, left_core)),
            (obuf.at[1, there], sib),
        )[way]
        return pltpu.make_async_remote_copy(
            src_ref=obuf.at[0, there],
            dst_ref=target,
            send_sem=fsend.at[p, way],
            recv_sem=frecv.at[p, way],
            device_id=(to, z),
            device_id_type=MESH,
        )

    for p in range(PIECES):
        own_copy(p).wait()
        for d in order:
            y_arrival(d, p).wait_recv()
        for way in range(3):
            forward(p, way).start()

    half = UNIT // 2

    def scores(left_unit, right_ref, n):
        return inner(left_unit, right_ref[n * half:(n + 1) * half])

    def wide(bias):
        return jnp.concatenate([bias] * (half // LANES), axis=1)

    def col_max(s, bias):
        return jnp.max(s + wide(bias), axis=0, keepdims=True)

    def row_max(s, bias_row, n):
        shifted = s + bias_row[:, n * half:(n + 1) * half]
        return jnp.maximum(shifted[:, :LANES], shifted[:, LANES:])

    def to_lanes(m):
        return jnp.max(m.T, axis=0, keepdims=True)

    own = obuf.at[0]
    own_unit = own[...]
    own_rows, own_lanes = row_bias(own_unit), lane_bias(own_unit)
    best = []
    for n in range(2):
        s = scores(own_unit, own, n)
        same = lax.broadcasted_iota(jnp.int32, s.shape, 0) == (
            lax.broadcasted_iota(jnp.int32, s.shape, 1) + n * half
        )
        best.append(col_max(jnp.where(same, jnp.float32(NEG), s), own_rows))
    own_best = jnp.concatenate(best, axis=1)

    for p in range(PIECES):
        forward(p, 2).wait_recv()
    sib_unit = obuf[1]
    sib_rows = row_bias(sib_unit)
    own_best = jnp.maximum(
        own_best,
        jnp.concatenate([col_max(scores(sib_unit, own, n), sib_rows) for n in range(2)], axis=1),
    )

    which = 1 - left // 2
    for p in range(PIECES):
        forward(p, 0).wait_recv()
    left_unit = lbuf[...]
    left_rows, left_lanes = row_bias(left_unit), lane_bias(left_unit)
    beside = obuf.at[which]
    beside_lanes = lane_bias(beside[...])
    best, left_acc = [], None
    for n in range(2):
        s = scores(left_unit, beside, n)
        best.append(col_max(s, left_rows))
        acc = row_max(s, beside_lanes, n)
        left_acc = acc if left_acc is None else jnp.maximum(left_acc, acc)
    beside_best = jnp.concatenate(best, axis=1)
    beside_own = which.astype(jnp.float32)
    own_best = jnp.maximum(own_best, beside_best + beside_own * NEG)
    sib_best = beside_best + (1.0 - beside_own) * NEG

    for p in range(PIECES):
        forward(p, 1).wait_recv()
    right_unit = rbuf[...]
    right_rows, right_lanes = row_bias(right_unit), lane_bias(right_unit)
    best, right_acc = [], None
    for n in range(2):
        s = scores(right_unit, own, n)
        best.append(col_max(s, right_rows))
        acc = row_max(s, own_lanes, n)
        right_acc = acc if right_acc is None else jnp.maximum(right_acc, acc)
    own_best = jnp.maximum(own_best, jnp.concatenate(best, axis=1))

    best = []
    for n in range(2):
        s = scores(left_unit, rbuf, n)
        best.append(col_max(s, left_rows))
        left_acc = jnp.maximum(left_acc, row_max(s, right_lanes, n))
    right_best = jnp.maximum(jnp.concatenate(best, axis=1), to_lanes(right_acc))
    left_best = to_lanes(left_acc)

    def give(way):
        to = (corpus_id(y, left, k), corpus_id(y, right, right_core), sib)[way]
        return pltpu.make_async_remote_copy(
            src_ref=part_out.at[way],
            dst_ref=part_in.at[way],
            send_sem=psend.at[way],
            recv_sem=precv.at[way],
            device_id=(to, z),
            device_id_type=MESH,
        )

    def as_tile(v):
        pieces = [v[:, i * LANES:(i + 1) * LANES] for i in range(UNIT // LANES)]
        return jnp.concatenate(pieces + [jnp.zeros((8 - len(pieces), LANES), jnp.float32)], axis=0)

    for way, v in ((1, right_best), (0, left_best), (2, sib_best)):
        part_out[way] = as_tile(v)
        give(way).start()
    final = jnp.maximum(as_tile(own_best), -1.0)
    for way in range(3):
        give(way).wait_recv()
        final = jnp.maximum(final, part_in[way])

    ret_y[y] = final

    def back_y(d, received):
        at = (y + NY - d) % NY if received else y
        return pltpu.make_async_remote_copy(
            src_ref=ret_y.at[at],
            dst_ref=ret_y.at[at],
            send_sem=ry_send.at[d],
            recv_sem=ry_recv.at[d],
            device_id=(corpus_id((y + d) % NY, x, k), z),
            device_id_type=MESH,
        )

    for d in order:
        back_y(d, False).start()
    for d in order:
        back_y(d, True).wait_recv()
    lane = lax.broadcasted_iota(jnp.int32, (NY, LANES), 1)
    mine = jnp.zeros((NY, LANES), jnp.float32)
    for p in range(PIECES):
        shift = (p * PIECE_RANKS - y * PIECE_RANKS + LANES) % LANES
        turned = pltpu.roll(ret_y[:, p, :], shift, 1)
        mine = jnp.where(lane // PIECE_RANKS == p, turned, mine)

    ret_z[z] = mine

    def back_z(d, received):
        at = (z + NZ - d) % NZ if received else z
        return pltpu.make_async_remote_copy(
            src_ref=ret_z.at[at],
            dst_ref=ret_z.at[at],
            send_sem=rz_send.at[d],
            recv_sem=rz_recv.at[d],
            device_id=(corpus, (z + d) % NZ),
            device_id_type=MESH,
        )

    for d in order:
        back_z(d, False).start()
    for d in order:
        back_z(d, True).wait_recv()

    table = ret_z[...].reshape(clusters, LANES)
    found = jnp.zeros((LANES, rows), jnp.float32)
    for _ in range(3):
        rounded = table.astype(jnp.bfloat16)
        table = table - rounded.astype(jnp.float32)
        found = found + lax.dot_general(
            rounded, onehot, (((0,), (0,)), ((), ())), preferred_element_type=jnp.float32
        )
    rank_i = lax.broadcasted_iota(jnp.int32, (SLOTS, rows), 0)
    hit = rank_i == rank.astype(jnp.int32)
    out_ref[...] = jnp.sum(jnp.where(hit, found[:SLOTS], 0.0), axis=0, keepdims=True)

    for p in range(PIECES):
        for d in order:
            y_copy(d, p).wait_send()
        for way in range(3):
            forward(p, way).wait_send()
    for way in range(3):
        give(way).wait_send()
    for d in order:
        back_y(d, False).wait_send()
        back_z(d, False).wait_send()


def local(embeddings, cluster_ids):
    rows, width = embeddings.shape
    dma = pltpu.SemaphoreType.DMA
    best = pl.pallas_call(
        kernel,
        out_shape=jax.ShapeDtypeStruct((1, rows), jnp.float32),
        in_specs=[pl.BlockSpec(memory_space=pl.ANY), pl.BlockSpec(memory_space=pltpu.VMEM)],
        out_specs=pl.BlockSpec(memory_space=pltpu.VMEM),
        scratch_shapes=[
            pltpu.VMEM((rows, width), jnp.bfloat16),
            pltpu.VMEM((PIECES, NY, PIECE_RANKS, width), jnp.bfloat16),
            pltpu.VMEM((2, UNIT, width), jnp.bfloat16),
            pltpu.VMEM((UNIT, width), jnp.bfloat16),
            pltpu.VMEM((UNIT, width), jnp.bfloat16),
            pltpu.VMEM((3, 8, LANES), jnp.float32),
            pltpu.VMEM((3, 8, LANES), jnp.float32),
            pltpu.VMEM((NY, 8, LANES), jnp.float32),
            pltpu.VMEM((NZ, NY, LANES), jnp.float32),
            dma,
            dma((PIECES,)),
            dma((PIECES, NY)), dma((PIECES, NY)),
            dma((PIECES, 3)), dma((PIECES, 3)),
            dma((3,)), dma((3,)),
            dma((NY,)), dma((NY,)),
            dma((NZ,)), dma((NZ,)),
        ],
        compiler_params=pltpu.CompilerParams(
            collective_id=0, has_side_effects=True, vmem_limit_bytes=48 * 2 ** 20
        ),
        name="cluster_best",
    )(embeddings, cluster_ids.reshape(1, rows))
    return best.reshape(rows)


def solution(mesh):
    in_specs = (P("corpus", None), P("corpus"))
    out_specs = P("corpus")
    return jax.shard_map(local, mesh=mesh, in_specs=in_specs, out_specs=out_specs, check_vma=False)
```

```python
import functools

import jax
import jax.numpy as jnp
from jax import lax
from jax.experimental import pallas as pl
from jax.experimental.pallas import tpu as pltpu
from jax.sharding import PartitionSpec as P

EPS = 1e-06
MESH = pl.DeviceIdType.MESH
NY, NX, NZ = 8, 4, 8
SLOTS = 64
PIECES = 4
PIECE_RANKS = SLOTS // PIECES
PIECE = NY * PIECE_RANKS
UNIT = NY * SLOTS
LANES = 128
MARK = 4.0
NEG = -1e6
HALF = UNIT // 2
SEND_ORDER = (4, 3, 5, 2, 6, 1, 7)
ARRIVAL_ORDER = SEND_ORDER


def corpus_id(y, x, k):
    return (y * NX + x) * 2 + k


def inner(left, right):
    return lax.dot_general(
        left, right, (((1,), (1,)), ((), ())), preferred_element_type=jnp.float32
    )


def row_bias(unit):
    head = unit[:, :LANES].astype(jnp.float32)
    return jnp.where(head > MARK / 2, jnp.float32(NEG), jnp.float32(0.0))


def lane_bias(unit):
    first = (lax.broadcasted_iota(jnp.int32, (16, LANES), 1) == 0).astype(jnp.bfloat16)
    head = inner(first, unit[:, :LANES])[0:1]
    return jnp.where(head > MARK / 2, jnp.float32(NEG), jnp.float32(0.0))


def kernel(
    emb_hbm, ids_hbm, out_ref,
    emb, ids_ref, counts, outbox, obuf, lbuf, rbuf, part_out, part_in, ret_y, ret_z,
    emb_sem, ids_sem, own_sem, ysend, yrecv, fsend, frecv, psend, precv,
    ry_send, ry_recv, rz_send, rz_recv,
):
    corpus = lax.axis_index("corpus")
    z = lax.axis_index("tile")
    y, x, k = corpus // (NX * 2), (corpus // 2) % NX, corpus % 2
    right, left = (x + 1) % NX, (x + NX - 1) % NX
    right_core = (k + x // 2) % 2
    left_core = (k + left // 2) % 2
    sib = corpus_id(y, x, 1 - k)
    rows, width = emb.shape

    ids_load = pltpu.make_async_copy(ids_hbm, ids_ref, ids_sem)
    ids_load.start()
    load = pltpu.make_async_copy(emb_hbm, emb, emb_sem)
    load.start()

    barrier = pltpu.get_barrier_semaphore()

    def greet(corpus_to, tile_to):
        pl.semaphore_signal(barrier, inc=1, device_id=(corpus_to, tile_to), device_id_type=MESH)

    for d in range(1, NY):
        greet(corpus_id((y + d) % NY, x, k), z)
    for core in range(2):
        greet(corpus_id(y, right, core), z)
        greet(corpus_id(y, left, core), z)
    greet(sib, z)
    for d in range(1, NZ):
        greet(corpus, (z + d) % NZ)

    ids_load.wait()
    ids = ids_ref[...]
    clusters = NY * NZ
    member = lax.broadcasted_iota(jnp.int32, (clusters, rows), 0) == ids
    onehot = jnp.where(member, jnp.float32(1.0), jnp.float32(0.0)).astype(jnp.bfloat16)
    step = 256
    row_i = lax.broadcasted_iota(jnp.int32, (step, step + LANES), 0)
    col_i = lax.broadcasted_iota(jnp.int32, (step, step + LANES), 1)
    earlier = ((row_i < col_i) | (col_i >= step)).astype(jnp.bfloat16)
    carry = jnp.zeros((clusters, LANES), jnp.float32)
    ranks = []
    for b in range(rows // step):
        part = onehot[:, b * step:(b + 1) * step]
        count = jnp.dot(part, earlier, preferred_element_type=jnp.float32)
        before = count[:, :step] + jnp.concatenate([carry] * (step // LANES), axis=1)
        ranks.append(jnp.sum(before * part.astype(jnp.float32), axis=0, keepdims=True))
        carry = carry + count[:, step:]
    rank = jnp.concatenate(ranks, axis=1)
    counts[...] = carry
    key = (ids - z * NY) * SLOTS + rank.astype(jnp.int32)

    def block_rows(p, source):
        return pl.ds(pl.multiple_of(p * PIECE + source * PIECE_RANKS, 16), PIECE_RANKS)

    def y_copy(d, p):
        to = (y + d) % NY
        return pltpu.make_async_remote_copy(
            src_ref=outbox.at[p, to],
            dst_ref=obuf.at[0, block_rows(p, y)],
            send_sem=ysend.at[p, d],
            recv_sem=yrecv.at[p, d],
            device_id=(corpus_id(to, x, k), z),
            device_id_type=MESH,
        )

    def y_arrival(d, p):
        source = (y + NY - d) % NY
        return pltpu.make_async_remote_copy(
            src_ref=outbox.at[p, source],
            dst_ref=obuf.at[0, block_rows(p, source)],
            send_sem=ysend.at[p, d],
            recv_sem=yrecv.at[p, d],
            device_id=(corpus_id(source, x, k), z),
            device_id_type=MESH,
        )

    def own_copy(p):
        return pltpu.make_async_copy(outbox.at[p, y], obuf.at[0, block_rows(p, y)], own_sem.at[p])

    def forward(p, way, source=None):
        there = pl.ds(p * PIECE, PIECE) if source is None else block_rows(p, source)
        target, to = (
            (lbuf.at[there], corpus_id(y, right, k)),
            (rbuf.at[there], corpus_id(y, left, left_core)),
            (obuf.at[1, there], sib),
        )[way]
        return pltpu.make_async_remote_copy(
            src_ref=obuf.at[0, there],
            dst_ref=target,
            send_sem=fsend.at[p, way],
            recv_sem=frecv.at[p, way],
            device_id=(to, z),
            device_id_type=MESH,
        )

    live = counts[pl.ds(pl.multiple_of(z * NY, 8), NY), :]
    live = jnp.broadcast_to(live[:, None, :], (NY, PIECE_RANKS, LANES)).reshape(PIECE, LANES)
    rank_i = (lax.broadcasted_iota(jnp.int32, (PIECE, LANES), 0) % PIECE_RANKS).astype(jnp.float32)
    slot_i = lax.broadcasted_iota(jnp.int32, (PIECE, 1), 0)
    load.wait()
    for p in range(PIECES):
        wanted = (slot_i // PIECE_RANKS) * SLOTS + p * PIECE_RANKS + slot_i % PIECE_RANKS
        pick = jnp.where(wanted == key, jnp.float32(1.0), jnp.float32(0.0)).astype(jnp.bfloat16)
        values = jnp.dot(pick, emb[...], preferred_element_type=jnp.float32)
        scale = lax.rsqrt(jnp.sum(values * values, axis=1, keepdims=True) + EPS)
        filled = rank_i + p * PIECE_RANKS < live
        head = jnp.where(filled, values[:, :LANES] * scale, jnp.float32(MARK))
        unit = jnp.concatenate([head, values[:, LANES:] * scale], axis=1)
        outbox[p] = unit.astype(jnp.bfloat16).reshape(NY, PIECE_RANKS, width)
        if p == 0:
            pl.semaphore_wait(barrier, NY - 1 + NZ - 1 + 5)
        for d in SEND_ORDER:
            y_copy(d, p).start()
        own_copy(p).start()

    for p in range(PIECES):
        own_copy(p).wait()
        for way in range(3):
            forward(p, way, y).start()
    for p in range(PIECES):
        for d in ARRIVAL_ORDER:
            y_arrival(d, p).wait_recv()
            for way in range(3):
                forward(p, way, (y + NY - d) % NY).start()

    def col_max(s, bias):
        bias = jnp.concatenate([bias] * (s.shape[1] // LANES), axis=1)
        return jnp.max(s + bias, axis=0, keepdims=True)

    def row_max(s, bias):
        s = s + bias
        best = s[:, :LANES]
        for i in range(1, s.shape[1] // LANES):
            best = jnp.maximum(best, s[:, i * LANES:(i + 1) * LANES])
        return best

    def to_lanes(m):
        return jnp.max(m.T, axis=0, keepdims=True)

    def half(ref, h):
        return ref[h * HALF:(h + 1) * HALF]

    def await_half(h, way):
        for p in range(h * PIECES // 2, (h + 1) * PIECES // 2):
            forward(p, way).wait_recv()

    own_unit = obuf[0]
    own_rows, own_lanes = row_bias(own_unit), lane_bias(own_unit)
    own_best = jnp.full((1, UNIT), NEG, jnp.float32)
    for h in range(2):
        s = inner(half(own_unit, h), own_unit)
        same = lax.broadcasted_iota(jnp.int32, s.shape, 0) + h * HALF == (
            lax.broadcasted_iota(jnp.int32, s.shape, 1)
        )
        best = col_max(jnp.where(same, jnp.float32(NEG), s), half(own_rows, h))
        own_best = jnp.maximum(own_best, best)

    for h in range(2):
        await_half(h, 2)
        sib_half = obuf[1, h * HALF:(h + 1) * HALF]
        best = col_max(inner(sib_half, own_unit), row_bias(sib_half))
        own_best = jnp.maximum(own_best, best)

    which = 1 - left // 2
    beside = obuf[which]
    beside_lanes = lane_bias(beside)
    beside_best = jnp.full((1, UNIT), NEG, jnp.float32)
    left_best, right_best, left_lanes, right_lanes = [], [], [], []
    for h in range(2):
        await_half(h, 0)
        left_half = half(lbuf, h)
        left_rows = row_bias(left_half)
        left_lanes.append(lane_bias(left_half))
        s = inner(left_half, beside)
        beside_best = jnp.maximum(beside_best, col_max(s, left_rows))
        left_acc = row_max(s, beside_lanes)

        await_half(h, 1)
        right_half = half(rbuf, h)
        right_rows = row_bias(right_half)
        right_lanes.append(lane_bias(right_half))
        s = inner(right_half, own_unit)
        own_best = jnp.maximum(own_best, col_max(s, right_rows))
        right_acc = row_max(s, own_lanes)

        s = inner(left_half, rbuf[:(h + 1) * HALF])
        left_acc = jnp.maximum(left_acc, row_max(s, jnp.concatenate(right_lanes, axis=1)))
        best = col_max(s, left_rows)
        for g in range(h):
            right_best[g] = jnp.maximum(right_best[g], best[:, g * HALF:(g + 1) * HALF])
        right_best.append(best[:, h * HALF:])
        if h > 0:
            s = inner(right_half, lbuf[:h * HALF])
            right_acc = jnp.maximum(right_acc, row_max(s, jnp.concatenate(left_lanes[:h], axis=1)))
            best = col_max(s, right_rows)
            for g in range(h):
                left_best[g] = jnp.maximum(left_best[g], best[:, g * HALF:(g + 1) * HALF])
        left_best.append(to_lanes(left_acc))
        right_best[h] = jnp.maximum(right_best[h], to_lanes(right_acc))
    left_best = jnp.concatenate(left_best, axis=1)
    right_best = jnp.concatenate(right_best, axis=1)
    beside_own = which.astype(jnp.float32)
    own_best = jnp.maximum(own_best, beside_best + beside_own * NEG)
    sib_best = beside_best + (1.0 - beside_own) * NEG

    def give(way):
        to = (corpus_id(y, left, k), corpus_id(y, right, right_core), sib)[way]
        return pltpu.make_async_remote_copy(
            src_ref=part_out.at[way],
            dst_ref=part_in.at[way],
            send_sem=psend.at[way],
            recv_sem=precv.at[way],
            device_id=(to, z),
            device_id_type=MESH,
        )

    def as_tile(v):
        pieces = [v[:, i * LANES:(i + 1) * LANES] for i in range(UNIT // LANES)]
        return jnp.concatenate(pieces + [jnp.zeros((8 - len(pieces), LANES), jnp.float32)], axis=0)

    for way, v in ((1, right_best), (0, left_best), (2, sib_best)):
        part_out[way] = as_tile(v)
        give(way).start()
    final = jnp.maximum(as_tile(own_best), -1.0)
    for way in range(3):
        give(way).wait_recv()
        final = jnp.maximum(final, part_in[way])

    ret_y[y] = final

    def back_y(d, received):
        at = (y + NY - d) % NY if received else y
        return pltpu.make_async_remote_copy(
            src_ref=ret_y.at[at],
            dst_ref=ret_y.at[at],
            send_sem=ry_send.at[d],
            recv_sem=ry_recv.at[d],
            device_id=(corpus_id((y + d) % NY, x, k), z),
            device_id_type=MESH,
        )

    for d in SEND_ORDER:
        back_y(d, False).start()
    for d in SEND_ORDER:
        back_y(d, True).wait_recv()
    lane = lax.broadcasted_iota(jnp.int32, (NY, LANES), 1)
    mine = jnp.zeros((NY, LANES), jnp.float32)
    for p in range(PIECES):
        shift = (p * PIECE_RANKS - y * PIECE_RANKS + LANES) % LANES
        turned = pltpu.roll(ret_y[:, p, :], shift, 1)
        mine = jnp.where(lane // PIECE_RANKS == p, turned, mine)

    ret_z[z] = mine

    def back_z(d, received):
        at = (z + NZ - d) % NZ if received else z
        return pltpu.make_async_remote_copy(
            src_ref=ret_z.at[at],
            dst_ref=ret_z.at[at],
            send_sem=rz_send.at[d],
            recv_sem=rz_recv.at[d],
            device_id=(corpus, (z + d) % NZ),
            device_id_type=MESH,
        )

    for d in SEND_ORDER:
        back_z(d, False).start()
    for d in SEND_ORDER:
        back_z(d, True).wait_recv()

    table = ret_z[...].reshape(clusters, LANES)
    found = jnp.zeros((LANES, rows), jnp.float32)
    for _ in range(3):
        rounded = table.astype(jnp.bfloat16)
        table = table - rounded.astype(jnp.float32)
        found = found + lax.dot_general(
            rounded, onehot, (((0,), (0,)), ((), ())), preferred_element_type=jnp.float32
        )
    rank_i = lax.broadcasted_iota(jnp.int32, (SLOTS, rows), 0)
    hit = rank_i == rank.astype(jnp.int32)
    out_ref[...] = jnp.sum(jnp.where(hit, found[:SLOTS], 0.0), axis=0, keepdims=True)

    for p in range(PIECES):
        for d in SEND_ORDER:
            y_copy(d, p).wait_send()
        for way in range(3):
            forward(p, way).wait_send()
    for way in range(3):
        give(way).wait_send()
    for d in SEND_ORDER:
        back_y(d, False).wait_send()
        back_z(d, False).wait_send()


def local(embeddings, cluster_ids):
    rows, width = embeddings.shape
    dma = pltpu.SemaphoreType.DMA
    best = pl.pallas_call(
        kernel,
        out_shape=jax.ShapeDtypeStruct((1, rows), jnp.float32),
        in_specs=[pl.BlockSpec(memory_space=pltpu.HBM)] * 2,
        out_specs=pl.BlockSpec(memory_space=pltpu.VMEM),
        scratch_shapes=[
            pltpu.VMEM((rows, width), jnp.bfloat16),
            pltpu.VMEM((1, rows), jnp.int32),
            pltpu.VMEM((NY * NZ, LANES), jnp.float32),
            pltpu.VMEM((PIECES, NY, PIECE_RANKS, width), jnp.bfloat16),
            pltpu.VMEM((2, UNIT, width), jnp.bfloat16),
            pltpu.VMEM((UNIT, width), jnp.bfloat16),
            pltpu.VMEM((UNIT, width), jnp.bfloat16),
            pltpu.VMEM((3, 8, LANES), jnp.float32),
            pltpu.VMEM((3, 8, LANES), jnp.float32),
            pltpu.VMEM((NY, 8, LANES), jnp.float32),
            pltpu.VMEM((NZ, NY, LANES), jnp.float32),
            dma, dma, dma((PIECES,)),
            dma((PIECES, NY)), dma((PIECES, NY)),
            dma((PIECES, 3)), dma((PIECES, 3)),
            dma((3,)), dma((3,)),
            dma((NY,)), dma((NY,)),
            dma((NZ,)), dma((NZ,)),
        ],
        compiler_params=pltpu.CompilerParams(
            collective_id=0, has_side_effects=True, vmem_limit_bytes=52 * 2 ** 20
        ),
        name="cluster_best",
    )(embeddings, cluster_ids.reshape(1, rows))
    return best.reshape(rows)


def solution(mesh):
    in_specs = (P("corpus", None), P("corpus"))
    out_specs = P("corpus")
    return jax.shard_map(local, mesh=mesh, in_specs=in_specs, out_specs=out_specs, check_vma=False)
```

```python
import functools

import jax
import jax.numpy as jnp
from jax import lax
from jax.experimental import pallas as pl
from jax.experimental.pallas import tpu as pltpu
from jax.sharding import PartitionSpec as P

EPS = 1e-06
MESH = pl.DeviceIdType.MESH
NY, NX, NZ = 8, 4, 8
SLOTS = 64
UNIT = NY * SLOTS
PIECE = 128
PIECES = UNIT // PIECE
FIRST = 3 * PIECE
LANES = 128
MARK = 4.0
NEG = -1e6
ORDER = (0, 1, 7, 2, 6, 3, 5, 4)
PLACE = {d: ORDER.index(d) for d in ORDER}
MESSAGES = (
    [(d, 0, 64) for d in (1, 7, 2, 6)]
    + [(d, at, 32) for at in (0, 32) for d in (3, 5)]
    + [(4, at, 16) for at in (0, 16, 32, 48)]
)


def corpus_id(y, x, k):
    return (y * NX + x) * 2 + k


def inner(left, right):
    return lax.dot_general(
        left, right, (((1,), (1,)), ((), ())), preferred_element_type=jnp.float32
    )


def row_bias(unit):
    head = unit[:, :LANES].astype(jnp.float32)
    return jnp.where(head > MARK / 2, jnp.float32(NEG), jnp.float32(0.0))


def lane_bias(unit):
    first = (lax.broadcasted_iota(jnp.int32, (16, LANES), 1) == 0).astype(jnp.bfloat16)
    head = inner(first, unit[:, :LANES])[0:1]
    return jnp.where(head > MARK / 2, jnp.float32(NEG), jnp.float32(0.0))


def kernel(
    emb_hbm, ids_hbm, out_ref,
    emb, ids_ref, counts, outbox, obuf, lbuf, rbuf, own_t, beside_t, left_t, right_t, part_out, part_in, ret_out, ret_in,
    emb_sem, ids_sem, ysend, yrecv, fsend, frecv, psend, precv,
    ret_send, ret_recv,
):
    corpus = lax.axis_index("corpus")
    z = lax.axis_index("tile")
    y, x, k = corpus // (NX * 2), (corpus // 2) % NX, corpus % 2
    right, left = (x + 1) % NX, (x + NX - 1) % NX
    right_core = (k + x // 2) % 2
    left_core = (k + left // 2) % 2
    sib = corpus_id(y, x, 1 - k)
    rows, width = emb.shape

    ids_load = pltpu.make_async_copy(ids_hbm, ids_ref, ids_sem)
    ids_load.start()
    load = pltpu.make_async_copy(emb_hbm, emb, emb_sem)
    load.start()

    barrier = pltpu.get_barrier_semaphore()

    def greet(corpus_to, tile_to):
        pl.semaphore_signal(barrier, inc=1, device_id=(corpus_to, tile_to), device_id_type=MESH)

    for d in range(1, NY):
        greet(corpus_id((y + d) % NY, x, k), z)
    for core in range(2):
        greet(corpus_id(y, right, core), z)
        greet(corpus_id(y, left, core), z)
    greet(sib, z)
    for d in range(1, NZ):
        greet(corpus, (z + d) % NZ)

    ids_load.wait()
    ids = ids_ref[...]
    clusters = NY * NZ
    member = lax.broadcasted_iota(jnp.int32, (clusters, rows), 0) == ids
    onehot = jnp.where(member, jnp.float32(1.0), jnp.float32(0.0)).astype(jnp.bfloat16)
    step = 256
    row_i = lax.broadcasted_iota(jnp.int32, (step, step + LANES), 0)
    col_i = lax.broadcasted_iota(jnp.int32, (step, step + LANES), 1)
    earlier = ((row_i < col_i) | (col_i >= step)).astype(jnp.bfloat16)
    carry = jnp.zeros((clusters, LANES), jnp.float32)
    ranks = []
    for b in range(rows // step):
        part = onehot[:, b * step:(b + 1) * step]
        count = jnp.dot(part, earlier, preferred_element_type=jnp.float32)
        before = count[:, :step] + jnp.concatenate([carry] * (step // LANES), axis=1)
        ranks.append(jnp.sum(before * part.astype(jnp.float32), axis=0, keepdims=True))
        carry = carry + count[:, step:]
    rank = jnp.concatenate(ranks, axis=1)
    counts[...] = carry
    key = (ids - z * NY) * SLOTS + rank.astype(jnp.int32)

    def y_copy(i):
        d, first, count = MESSAGES[i]
        return pltpu.make_async_remote_copy(
            src_ref=outbox.at[d, pl.ds(first, count)],
            dst_ref=obuf.at[0, pl.ds(PLACE[d] * SLOTS + first, count)],
            send_sem=ysend,
            recv_sem=yrecv.at[i],
            device_id=(corpus_id((y + d) % NY, x, k), z),
            device_id_type=MESH,
        )

    def forward(way, first, count):
        there = pl.ds(first, count)
        target, to = (
            (lbuf.at[there], corpus_id(y, right, k)),
            (rbuf.at[there], corpus_id(y, left, left_core)),
            (obuf.at[1, there], sib),
        )[way]
        return pltpu.make_async_remote_copy(
            src_ref=obuf.at[0, there],
            dst_ref=target,
            send_sem=fsend.at[way],
            recv_sem=frecv.at[first // FIRST, way],
            device_id=(to, z),
            device_id_type=MESH,
        )

    slot_i = lax.broadcasted_iota(jnp.int32, (2 * SLOTS, 1), 0)
    rank_i = lax.broadcasted_iota(jnp.int32, (SLOTS, LANES), 0).astype(jnp.float32)
    load.wait()
    for pair in range(NY // 2):
        dists = ORDER[2 * pair:2 * pair + 2]
        tos = [(y + d) % NY for d in dists]
        wanted = slot_i % SLOTS + SLOTS * jnp.where(slot_i < SLOTS, tos[0], tos[1])
        pick = jnp.where(wanted == key, jnp.float32(1.0), jnp.float32(0.0)).astype(jnp.bfloat16)
        values = jnp.dot(pick, emb[...], preferred_element_type=jnp.float32)
        scale = lax.rsqrt(jnp.sum(values * values, axis=1, keepdims=True) + EPS)
        filled = jnp.concatenate([rank_i < counts[pl.ds(z * NY + to, 1), :] for to in tos], axis=0)
        head = jnp.where(filled, values[:, :LANES] * scale, jnp.float32(MARK))
        unit = jnp.concatenate([head, values[:, LANES:] * scale], axis=1).astype(jnp.bfloat16)
        for i, d in enumerate(dists):
            if d == 0:
                obuf[0, :SLOTS] = unit[i * SLOTS:(i + 1) * SLOTS]
            else:
                outbox[d] = unit[i * SLOTS:(i + 1) * SLOTS]
        if pair == 0:
            pl.semaphore_wait(barrier, NY - 1 + NZ - 1 + 5)
        for i, message in enumerate(MESSAGES):
            if message[0] in dists:
                y_copy(i).start()
        if pair == 0:
            for way in range(3):
                forward(way, 0, SLOTS).start()

    for i, (d, first, count) in enumerate(MESSAGES):
        y_copy(i).wait_recv()
        for way in range(3):
            forward(way, PLACE[d] * SLOTS + first, count).start()

    def col_max(s, bias):
        bias = jnp.concatenate([bias] * (s.shape[1] // LANES), axis=1)
        return jnp.max(s + bias, axis=0, keepdims=True)

    def row_max(s, bias):
        s = s + bias
        best = s[:, :LANES]
        for i in range(1, s.shape[1] // LANES):
            best = jnp.maximum(best, s[:, i * LANES:(i + 1) * LANES])
        return best

    def to_lanes(m):
        return jnp.max(m.T, axis=0, keepdims=True)

    def piece(ref, p):
        return ref[p * PIECE:(p + 1) * PIECE]

    def dot(left, right):
        return jnp.dot(left, right, preferred_element_type=jnp.float32)

    def await_part(part, way):
        forward(way, part * FIRST, UNIT - FIRST if part else FIRST).wait_recv()

    own_unit = obuf[0]
    own_rows, own_lanes = row_bias(own_unit), lane_bias(own_unit)
    for p in range(PIECES):
        own_t[:, p * PIECE:(p + 1) * PIECE] = piece(own_unit, p).T
    own_best = jnp.full((1, UNIT), NEG, jnp.float32)
    for p in range(PIECES):
        s = dot(piece(own_unit, p), own_t[...])
        same = lax.broadcasted_iota(jnp.int32, s.shape, 0) + p * PIECE == (
            lax.broadcasted_iota(jnp.int32, s.shape, 1)
        )
        best = col_max(jnp.where(same, jnp.float32(NEG), s), piece(own_rows, p))
        own_best = jnp.maximum(own_best, best)

    await_part(0, 2)
    await_part(1, 2)
    which = 1 - left // 2
    beside = obuf[which]
    beside_lanes = lane_bias(beside)
    for p in range(PIECES):
        beside_t[:, p * PIECE:(p + 1) * PIECE] = piece(beside, p).T
        sib_piece = obuf[1, p * PIECE:(p + 1) * PIECE]
        best = col_max(dot(sib_piece, own_t[...]), row_bias(sib_piece))
        own_best = jnp.maximum(own_best, best)

    beside_best = jnp.full((1, UNIT), NEG, jnp.float32)
    left_best, right_best, left_lanes, right_lanes = [], [], [], []
    for p in range(PIECES):
        there = slice(p * PIECE, (p + 1) * PIECE)
        if p * PIECE in (0, FIRST):
            await_part(p * PIECE // FIRST, 0)
            await_part(p * PIECE // FIRST, 1)
        left_piece, right_piece = lbuf[there], rbuf[there]
        left_rows, right_rows = row_bias(left_piece), row_bias(right_piece)
        left_lanes.append(lane_bias(left_piece))
        right_lanes.append(lane_bias(right_piece))
        right_t[:, there] = right_piece.T
        if p < PIECES - 1:
            left_t[:, there] = left_piece.T
        s = dot(left_piece, beside_t[...])
        beside_best = jnp.maximum(beside_best, col_max(s, left_rows))
        left_acc = row_max(s, beside_lanes)

        s = dot(right_piece, own_t[...])
        own_best = jnp.maximum(own_best, col_max(s, right_rows))
        right_acc = row_max(s, own_lanes)

        s = dot(left_piece, right_t[:, :(p + 1) * PIECE])
        left_acc = jnp.maximum(left_acc, row_max(s, jnp.concatenate(right_lanes, axis=1)))
        best = col_max(s, left_rows)
        for q in range(p):
            right_best[q] = jnp.maximum(right_best[q], best[:, q * PIECE:(q + 1) * PIECE])
        right_best.append(best[:, p * PIECE:])
        if p > 0:
            s = dot(right_piece, left_t[:, :p * PIECE])
            right_acc = jnp.maximum(right_acc, row_max(s, jnp.concatenate(left_lanes[:p], axis=1)))
            best = col_max(s, right_rows)
            for q in range(p):
                left_best[q] = jnp.maximum(left_best[q], best[:, q * PIECE:(q + 1) * PIECE])
        left_best.append(to_lanes(left_acc))
        right_best[p] = jnp.maximum(right_best[p], to_lanes(right_acc))
    left_best = jnp.concatenate(left_best, axis=1)
    right_best = jnp.concatenate(right_best, axis=1)
    beside_own = which.astype(jnp.float32)
    own_best = jnp.maximum(own_best, beside_best + beside_own * NEG)
    sib_best = beside_best + (1.0 - beside_own) * NEG

    def give(way):
        to = (corpus_id(y, left, k), corpus_id(y, right, right_core), sib)[way]
        return pltpu.make_async_remote_copy(
            src_ref=part_out.at[way],
            dst_ref=part_in.at[way],
            send_sem=psend,
            recv_sem=precv,
            device_id=(to, z),
            device_id_type=MESH,
        )

    def as_tile(v):
        pieces = [v[:, i * LANES:(i + 1) * LANES] for i in range(UNIT // LANES)]
        return jnp.concatenate(pieces + [jnp.zeros((8 - len(pieces), LANES), jnp.float32)], axis=0)

    for way, v in ((1, right_best), (0, left_best), (2, sib_best)):
        part_out[way] = as_tile(v)
        give(way).start()
    final = jnp.maximum(as_tile(own_best), -1.0)

    def whole(ref, send_sem, recv_sem):
        return pltpu.make_async_remote_copy(
            src_ref=ref, dst_ref=ref, send_sem=send_sem, recv_sem=recv_sem,
            device_id=(sib, z), device_id_type=MESH,
        )

    whole(part_in, psend, precv).wait_recv()
    for way in range(3):
        final = jnp.maximum(final, part_in[way])

    home = z * NY + y
    for d in range(NY):
        row = final[PLACE[d] // 2:PLACE[d] // 2 + 1]
        if PLACE[d] % 2:
            row = jnp.concatenate([row[:, SLOTS:], row[:, :SLOTS]], axis=1)
        ret_out[d] = row
        if d == 0:
            ret_in[home] = row
    hops = [(d, e) for d in range(NY) for e in range(NZ) if d or e]
    hops.sort(key=lambda de: -min(de[0], NY - de[0]) - min(de[1], NZ - de[1]))
    for d, e in hops:
        pltpu.make_async_remote_copy(
            src_ref=ret_out.at[d],
            dst_ref=ret_in.at[home],
            send_sem=ret_send,
            recv_sem=ret_recv,
            device_id=(corpus_id((y + NY - d) % NY, x, k), (z + e) % NZ),
            device_id_type=MESH,
        ).start()
    returned = whole(ret_in.at[pl.ds(0, NY * NZ - 1)], ret_send, ret_recv)
    returned.wait_recv()

    table = ret_in[...].reshape(clusters, LANES)[:, :SLOTS]
    found = jnp.zeros((SLOTS, rows), jnp.float32)
    for _ in range(3):
        rounded = table.astype(jnp.bfloat16)
        table = table - rounded.astype(jnp.float32)
        found = found + lax.dot_general(
            rounded, onehot, (((0,), (0,)), ((), ())), preferred_element_type=jnp.float32
        )
    rank_i = lax.broadcasted_iota(jnp.int32, (SLOTS, rows), 0)
    hit = rank_i == rank.astype(jnp.int32)
    out_ref[...] = jnp.sum(jnp.where(hit, found, 0.0), axis=0, keepdims=True)

    whole(outbox.at[pl.ds(1, NY - 1)], ysend, ysend).wait_send()
    for way in range(3):
        whole(obuf.at[0], fsend.at[way], fsend.at[way]).wait_send()
    whole(part_out, psend, precv).wait_send()
    returned.wait_send()


def local(embeddings, cluster_ids):
    rows, width = embeddings.shape
    dma = pltpu.SemaphoreType.DMA
    best = pl.pallas_call(
        kernel,
        out_shape=jax.ShapeDtypeStruct((1, rows), jnp.float32),
        in_specs=[pl.BlockSpec(memory_space=pltpu.HBM)] * 2,
        out_specs=pl.BlockSpec(memory_space=pltpu.VMEM),
        scratch_shapes=[
            pltpu.VMEM((rows, width), jnp.bfloat16),
            pltpu.VMEM((1, rows), jnp.int32),
            pltpu.VMEM((NY * NZ, LANES), jnp.float32),
            pltpu.VMEM((NY, SLOTS, width), jnp.bfloat16),
            pltpu.VMEM((2, UNIT, width), jnp.bfloat16),
            pltpu.VMEM((UNIT, width), jnp.bfloat16),
            pltpu.VMEM((UNIT, width), jnp.bfloat16),
            *[pltpu.VMEM((width, UNIT), jnp.bfloat16)] * 4,
            pltpu.VMEM((3, 8, LANES), jnp.float32),
            pltpu.VMEM((3, 8, LANES), jnp.float32),
            pltpu.VMEM((NY, 1, LANES), jnp.float32),
            pltpu.VMEM((NY * NZ, 1, LANES), jnp.float32),
            dma, dma,
            dma, dma((len(MESSAGES),)),
            dma((3,)), dma((2, 3)),
            dma, dma, dma, dma,
        ],
        compiler_params=pltpu.CompilerParams(
            collective_id=0, has_side_effects=True, vmem_limit_bytes=52 * 2 ** 20
        ),
        name="cluster_best",
    )(embeddings, cluster_ids.reshape(1, rows))
    return best.reshape(rows)


def solution(mesh):
    in_specs = (P("corpus", None), P("corpus"))
    out_specs = P("corpus")
    return jax.shard_map(local, mesh=mesh, in_specs=in_specs, out_specs=out_specs, check_vma=False)
```

```python
import functools

import jax
import jax.numpy as jnp
from jax import lax
from jax.experimental import pallas as pl
from jax.experimental.pallas import tpu as pltpu
from jax.sharding import PartitionSpec as P

EPS = 1e-06
MESH = pl.DeviceIdType.MESH
NY, NX, NZ = 8, 4, 8
SLOTS = 64
UNIT = NY * SLOTS
PIECE = 128
PIECES = UNIT // PIECE
FIRST = 3 * PIECE
LANES = 128
MARK = 4.0
NEG = -1e6
ORDER = (0, 1, 7, 2, 6, 3, 5, 4)
PLACE = {d: ORDER.index(d) for d in ORDER}
MESSAGES = (
    [(d, 0, 64) for d in (1, 7, 2, 6)]
    + [(d, at, 32) for at in (0, 32) for d in (3, 5)]
    + [(4, at, 16) for at in (0, 16, 32, 48)]
)


def corpus_id(y, x, k):
    return (y * NX + x) * 2 + k


def inner(left, right):
    return lax.dot_general(
        left, right, (((1,), (1,)), ((), ())), preferred_element_type=jnp.float32
    )


def row_bias(unit):
    head = unit[:, :LANES].astype(jnp.float32)
    return jnp.where(head > MARK / 2, jnp.float32(NEG), jnp.float32(0.0))


def lane_bias(unit):
    first = (lax.broadcasted_iota(jnp.int32, (16, LANES), 1) == 0).astype(jnp.bfloat16)
    head = inner(first, unit[:, :LANES])[0:1]
    return jnp.where(head > MARK / 2, jnp.float32(NEG), jnp.float32(0.0))


def kernel(
    emb_hbm, ids_hbm, out_ref,
    emb, ids_ref, counts, outbox, obuf, lbuf, rbuf, own_t, beside_t, left_t, right_t, part_out, part_in, ret_out, ret_in,
    emb_sem, ids_sem, ysend, yrecv, fsend, frecv, psend, precv,
    ret_send, ret_recv,
):
    corpus = lax.axis_index("corpus")
    z = lax.axis_index("tile")
    y, x, k = corpus // (NX * 2), (corpus // 2) % NX, corpus % 2
    right, left = (x + 1) % NX, (x + NX - 1) % NX
    right_core = (k + x // 2) % 2
    left_core = (k + left // 2) % 2
    sib = corpus_id(y, x, 1 - k)
    rows, width = emb.shape

    ids_load = pltpu.make_async_copy(ids_hbm, ids_ref, ids_sem)
    ids_load.start()
    load = pltpu.make_async_copy(emb_hbm, emb, emb_sem)
    load.start()

    barrier = pltpu.get_barrier_semaphore()

    def greet(corpus_to, tile_to):
        pl.semaphore_signal(barrier, inc=1, device_id=(corpus_to, tile_to), device_id_type=MESH)

    for d in range(1, NY):
        greet(corpus_id((y + d) % NY, x, k), z)
    for core in range(2):
        greet(corpus_id(y, right, core), z)
        greet(corpus_id(y, left, core), z)
    greet(sib, z)
    for d in range(1, NZ):
        greet(corpus, (z + d) % NZ)

    ids_load.wait()
    ids = ids_ref[...]
    clusters = NY * NZ
    member = lax.broadcasted_iota(jnp.int32, (clusters, rows), 0) == ids
    onehot = jnp.where(member, jnp.float32(1.0), jnp.float32(0.0)).astype(jnp.bfloat16)
    step = 256
    row_i = lax.broadcasted_iota(jnp.int32, (step, step + LANES), 0)
    col_i = lax.broadcasted_iota(jnp.int32, (step, step + LANES), 1)
    earlier = ((row_i < col_i) | (col_i >= step)).astype(jnp.bfloat16)
    carry = jnp.zeros((clusters, LANES), jnp.float32)
    ranks = []
    for b in range(rows // step):
        part = onehot[:, b * step:(b + 1) * step]
        count = jnp.dot(part, earlier, preferred_element_type=jnp.float32)
        before = count[:, :step] + jnp.concatenate([carry] * (step // LANES), axis=1)
        ranks.append(jnp.sum(before * part.astype(jnp.float32), axis=0, keepdims=True))
        carry = carry + count[:, step:]
    rank = jnp.concatenate(ranks, axis=1)
    counts[...] = carry
    key = (ids - z * NY) * SLOTS + rank.astype(jnp.int32)

    def y_copy(i):
        d, first, count = MESSAGES[i]
        return pltpu.make_async_remote_copy(
            src_ref=outbox.at[d, pl.ds(first, count)],
            dst_ref=obuf.at[0, pl.ds(PLACE[d] * SLOTS + first, count)],
            send_sem=ysend,
            recv_sem=yrecv.at[i],
            device_id=(corpus_id((y + d) % NY, x, k), z),
            device_id_type=MESH,
        )

    def forward(way, first, count):
        there = pl.ds(first, count)
        target, to = (
            (lbuf.at[there], corpus_id(y, right, k)),
            (rbuf.at[there], corpus_id(y, left, left_core)),
            (obuf.at[1, there], sib),
        )[way]
        return pltpu.make_async_remote_copy(
            src_ref=obuf.at[0, there],
            dst_ref=target,
            send_sem=fsend.at[way],
            recv_sem=frecv.at[first // FIRST, way],
            device_id=(to, z),
            device_id_type=MESH,
        )

    slot_i = lax.broadcasted_iota(jnp.int32, (2 * SLOTS, 1), 0)
    rank_i = lax.broadcasted_iota(jnp.int32, (SLOTS, LANES), 0).astype(jnp.float32)
    load.wait()
    for pair in range(NY // 2):
        dists = ORDER[2 * pair:2 * pair + 2]
        tos = [(y + d) % NY for d in dists]
        wanted = slot_i % SLOTS + SLOTS * jnp.where(slot_i < SLOTS, tos[0], tos[1])
        pick = jnp.where(wanted == key, jnp.float32(1.0), jnp.float32(0.0)).astype(jnp.bfloat16)
        values = jnp.dot(pick, emb[...], preferred_element_type=jnp.float32)
        scale = lax.rsqrt(jnp.sum(values * values, axis=1, keepdims=True) + EPS)
        filled = jnp.concatenate([rank_i < counts[pl.ds(z * NY + to, 1), :] for to in tos], axis=0)
        head = jnp.where(filled, values[:, :LANES] * scale, jnp.float32(MARK))
        unit = jnp.concatenate([head, values[:, LANES:] * scale], axis=1).astype(jnp.bfloat16)
        for i, d in enumerate(dists):
            if d == 0:
                obuf[0, :SLOTS] = unit[i * SLOTS:(i + 1) * SLOTS]
            else:
                outbox[d] = unit[i * SLOTS:(i + 1) * SLOTS]
        if pair == 0:
            pl.semaphore_wait(barrier, NY - 1 + NZ - 1 + 5)
        for i, message in enumerate(MESSAGES):
            if message[0] in dists:
                y_copy(i).start()
        if pair == 0:
            for way in range(3):
                forward(way, 0, SLOTS).start()

    for i, (d, first, count) in enumerate(MESSAGES):
        y_copy(i).wait_recv()
        for way in range(3):
            forward(way, PLACE[d] * SLOTS + first, count).start()

    def col_max(s, bias):
        bias = jnp.concatenate([bias] * (s.shape[1] // LANES), axis=1)
        return jnp.max(s + bias, axis=0, keepdims=True)

    def row_max(s, bias):
        s = s + bias
        best = s[:, :LANES]
        for i in range(1, s.shape[1] // LANES):
            best = jnp.maximum(best, s[:, i * LANES:(i + 1) * LANES])
        return best

    def to_lanes(m):
        return jnp.max(m.T, axis=0, keepdims=True)

    def piece(ref, p):
        return ref[p * PIECE:(p + 1) * PIECE]

    def dot(left, right):
        return jnp.dot(left, right, preferred_element_type=jnp.float32)

    def await_part(part, way):
        forward(way, part * FIRST, UNIT - FIRST if part else FIRST).wait_recv()

    own_unit = obuf[0]
    own_rows, own_lanes = row_bias(own_unit), lane_bias(own_unit)
    for p in range(PIECES):
        own_t[:, p * PIECE:(p + 1) * PIECE] = piece(own_unit, p).T
    own_best = jnp.full((1, UNIT), NEG, jnp.float32)
    for p in range(PIECES):
        s = dot(piece(own_unit, p), own_t[...])
        same = lax.broadcasted_iota(jnp.int32, s.shape, 0) + p * PIECE == (
            lax.broadcasted_iota(jnp.int32, s.shape, 1)
        )
        best = col_max(jnp.where(same, jnp.float32(NEG), s), piece(own_rows, p))
        own_best = jnp.maximum(own_best, best)

    await_part(0, 2)
    await_part(1, 2)
    which = 1 - left // 2
    beside = obuf[which]
    beside_lanes = lane_bias(beside)
    for p in range(PIECES):
        beside_t[:, p * PIECE:(p + 1) * PIECE] = piece(beside, p).T
        sib_piece = obuf[1, p * PIECE:(p + 1) * PIECE]
        best = col_max(dot(sib_piece, own_t[...]), row_bias(sib_piece))
        own_best = jnp.maximum(own_best, best)

    beside_best = jnp.full((1, UNIT), NEG, jnp.float32)
    left_best, right_best, left_lanes, right_lanes = [], [], [], []
    for p in range(PIECES):
        there = slice(p * PIECE, (p + 1) * PIECE)
        if p * PIECE in (0, FIRST):
            await_part(p * PIECE // FIRST, 0)
            await_part(p * PIECE // FIRST, 1)
        left_piece, right_piece = lbuf[there], rbuf[there]
        left_rows, right_rows = row_bias(left_piece), row_bias(right_piece)
        left_lanes.append(lane_bias(left_piece))
        right_lanes.append(lane_bias(right_piece))
        right_t[:, there] = right_piece.T
        if p < PIECES - 1:
            left_t[:, there] = left_piece.T
        s = dot(left_piece, beside_t[...])
        beside_best = jnp.maximum(beside_best, col_max(s, left_rows))
        left_acc = row_max(s, beside_lanes)

        s = dot(right_piece, own_t[...])
        own_best = jnp.maximum(own_best, col_max(s, right_rows))
        right_acc = row_max(s, own_lanes)

        s = dot(left_piece, right_t[:, :(p + 1) * PIECE])
        left_acc = jnp.maximum(left_acc, row_max(s, jnp.concatenate(right_lanes, axis=1)))
        best = col_max(s, left_rows)
        for q in range(p):
            right_best[q] = jnp.maximum(right_best[q], best[:, q * PIECE:(q + 1) * PIECE])
        right_best.append(best[:, p * PIECE:])
        if p > 0:
            s = dot(right_piece, left_t[:, :p * PIECE])
            right_acc = jnp.maximum(right_acc, row_max(s, jnp.concatenate(left_lanes[:p], axis=1)))
            best = col_max(s, right_rows)
            for q in range(p):
                left_best[q] = jnp.maximum(left_best[q], best[:, q * PIECE:(q + 1) * PIECE])
        left_best.append(to_lanes(left_acc))
        right_best[p] = jnp.maximum(right_best[p], to_lanes(right_acc))
    left_best = jnp.concatenate(left_best, axis=1)
    right_best = jnp.concatenate(right_best, axis=1)
    beside_own = which.astype(jnp.float32)
    own_best = jnp.maximum(own_best, beside_best + beside_own * NEG)
    sib_best = beside_best + (1.0 - beside_own) * NEG

    def give(way):
        to = (corpus_id(y, left, k), corpus_id(y, right, right_core), sib)[way]
        return pltpu.make_async_remote_copy(
            src_ref=part_out.at[way],
            dst_ref=part_in.at[way],
            send_sem=psend,
            recv_sem=precv,
            device_id=(to, z),
            device_id_type=MESH,
        )

    def as_tile(v):
        pieces = [v[:, i * LANES:(i + 1) * LANES] for i in range(UNIT // LANES)]
        return jnp.concatenate(pieces + [jnp.zeros((8 - len(pieces), LANES), jnp.float32)], axis=0)

    for way, v in ((1, right_best), (0, left_best), (2, sib_best)):
        part_out[way] = as_tile(v)
        give(way).start()
    final = jnp.maximum(as_tile(own_best), -1.0)

    def whole(ref, send_sem, recv_sem):
        return pltpu.make_async_remote_copy(
            src_ref=ref, dst_ref=ref, send_sem=send_sem, recv_sem=recv_sem,
            device_id=(sib, z), device_id_type=MESH,
        )

    whole(part_in, psend, precv).wait_recv()
    for way in range(3):
        final = jnp.maximum(final, part_in[way])

    home = z * NY + y
    for d in range(NY):
        row = final[PLACE[d] // 2:PLACE[d] // 2 + 1]
        if PLACE[d] % 2:
            row = jnp.concatenate([row[:, SLOTS:], row[:, :SLOTS]], axis=1)
        ret_out[(y + NY - d) % NY] = row
        if d == 0:
            ret_in[home] = row
    for i in range(NY * NZ - 1):
        to = i + (i + NY * NZ - home) // (NY * NZ)
        pltpu.make_async_remote_copy(
            src_ref=ret_out.at[to % NY],
            dst_ref=ret_in.at[home],
            send_sem=ret_send,
            recv_sem=ret_recv,
            device_id=(corpus_id(to % NY, x, k), to // NY),
            device_id_type=MESH,
        ).start()
    returned = whole(ret_in.at[pl.ds(0, NY * NZ - 1)], ret_send, ret_recv)
    returned.wait_recv()

    table = ret_in[...].reshape(clusters, LANES)[:, :SLOTS]
    found = jnp.zeros((SLOTS, rows), jnp.float32)
    for _ in range(3):
        rounded = table.astype(jnp.bfloat16)
        table = table - rounded.astype(jnp.float32)
        found = found + lax.dot_general(
            rounded, onehot, (((0,), (0,)), ((), ())), preferred_element_type=jnp.float32
        )
    rank_i = lax.broadcasted_iota(jnp.int32, (SLOTS, rows), 0)
    hit = rank_i == rank.astype(jnp.int32)
    out_ref[...] = jnp.sum(jnp.where(hit, found, 0.0), axis=0, keepdims=True)

    whole(outbox.at[pl.ds(1, NY - 1)], ysend, ysend).wait_send()
    for way in range(3):
        whole(obuf.at[0], fsend.at[way], fsend.at[way]).wait_send()
    whole(part_out, psend, precv).wait_send()
    returned.wait_send()


def local(embeddings, cluster_ids):
    rows, width = embeddings.shape
    dma = pltpu.SemaphoreType.DMA
    best = pl.pallas_call(
        kernel,
        out_shape=jax.ShapeDtypeStruct((1, rows), jnp.float32),
        in_specs=[pl.BlockSpec(memory_space=pltpu.HBM)] * 2,
        out_specs=pl.BlockSpec(memory_space=pltpu.VMEM),
        scratch_shapes=[
            pltpu.VMEM((rows, width), jnp.bfloat16),
            pltpu.VMEM((1, rows), jnp.int32),
            pltpu.VMEM((NY * NZ, LANES), jnp.float32),
            pltpu.VMEM((NY, SLOTS, width), jnp.bfloat16),
            pltpu.VMEM((2, UNIT, width), jnp.bfloat16),
            pltpu.VMEM((UNIT, width), jnp.bfloat16),
            pltpu.VMEM((UNIT, width), jnp.bfloat16),
            *[pltpu.VMEM((width, UNIT), jnp.bfloat16)] * 4,
            pltpu.VMEM((3, 8, LANES), jnp.float32),
            pltpu.VMEM((3, 8, LANES), jnp.float32),
            pltpu.VMEM((NY, 1, LANES), jnp.float32),
            pltpu.VMEM((NY * NZ, 1, LANES), jnp.float32),
            dma, dma,
            dma, dma((len(MESSAGES),)),
            dma((3,)), dma((2, 3)),
            dma, dma, dma, dma,
        ],
        compiler_params=pltpu.CompilerParams(
            collective_id=0, has_side_effects=True, vmem_limit_bytes=55222 * 2 ** 10
        ),
        name="cluster_best",
    )(embeddings, cluster_ids.reshape(1, rows))
    return best.reshape(rows)


def solution(mesh):
    in_specs = (P("corpus", None), P("corpus"))
    out_specs = P("corpus")
    return jax.shard_map(local, mesh=mesh, in_specs=in_specs, out_specs=out_specs, check_vma=False)
```

```python
import functools

import jax
import jax.numpy as jnp
from jax import lax
from jax.experimental import pallas as pl
from jax.experimental.pallas import tpu as pltpu
from jax.sharding import PartitionSpec as P

EPS = 1e-06
MESH = pl.DeviceIdType.MESH
NY, NX, NZ = 8, 4, 8
SLOTS = 64
UNIT = NY * SLOTS
PIECE = 128
PIECES = UNIT // PIECE
FIRST = 3 * PIECE
LANES = 128
MARK = 4.0
NEG = -1e6
ORDER = (0, 1, 7, 2, 6, 3, 5, 4)
PLACE = {d: ORDER.index(d) for d in ORDER}
MESSAGES = (
    [(d, 0, 64) for d in (1, 7, 2, 6)]
    + [(d, at, 32) for at in (0, 32) for d in (3, 5)]
    + [(4, at, 16) for at in (0, 16, 32, 48)]
)


def corpus_id(y, x, k):
    return (y * NX + x) * 2 + k


def inner(left, right):
    return lax.dot_general(
        left, right, (((1,), (1,)), ((), ())), preferred_element_type=jnp.float32
    )


def row_bias(unit):
    head = unit[:, :LANES].astype(jnp.float32)
    return jnp.where(head > MARK / 2, jnp.float32(NEG), jnp.float32(0.0))


def lane_bias(unit):
    first = (lax.broadcasted_iota(jnp.int32, (16, LANES), 1) == 0).astype(jnp.bfloat16)
    head = inner(first, unit[:, :LANES])[0:1]
    return jnp.where(head > MARK / 2, jnp.float32(NEG), jnp.float32(0.0))


def kernel(
    emb_hbm, ids_hbm, out_ref,
    emb, ids_ref, counts, thrice, outbox, obuf, lbuf, rbuf, own_t, beside_t, left_t, right_t, part_out, part_in, ret_out, ret_in,
    emb_sem, ids_sem, ysend, yrecv, fsend, frecv, psend, precv,
    ret_send, ret_recv,
):
    corpus = lax.axis_index("corpus")
    z = lax.axis_index("tile")
    y, x, k = corpus // (NX * 2), (corpus // 2) % NX, corpus % 2
    right, left = (x + 1) % NX, (x + NX - 1) % NX
    right_core = (k + x // 2) % 2
    left_core = (k + left // 2) % 2
    sib = corpus_id(y, x, 1 - k)
    rows, width = emb.shape

    ids_load = pltpu.make_async_copy(ids_hbm, ids_ref, ids_sem)
    ids_load.start()
    load = pltpu.make_async_copy(emb_hbm, emb, emb_sem)
    load.start()

    barrier = pltpu.get_barrier_semaphore()

    def greet(corpus_to, tile_to):
        pl.semaphore_signal(barrier, inc=1, device_id=(corpus_to, tile_to), device_id_type=MESH)

    for d in range(1, NY):
        greet(corpus_id((y + d) % NY, x, k), z)
    for core in range(2):
        greet(corpus_id(y, right, core), z)
        greet(corpus_id(y, left, core), z)
    greet(sib, z)
    for d in range(1, NZ):
        greet(corpus, (z + d) % NZ)

    ids_load.wait()
    ids = ids_ref[...]
    clusters = NY * NZ
    member = lax.broadcasted_iota(jnp.int32, (clusters, rows), 0) == ids
    onehot = jnp.where(member, jnp.float32(1.0), jnp.float32(0.0)).astype(jnp.bfloat16)
    for i in range(3):
        thrice[i * clusters:(i + 1) * clusters] = onehot
    step = 256
    row_i = lax.broadcasted_iota(jnp.int32, (step, step + LANES), 0)
    col_i = lax.broadcasted_iota(jnp.int32, (step, step + LANES), 1)
    earlier = ((row_i < col_i) | (col_i >= step)).astype(jnp.bfloat16)
    carry = jnp.zeros((clusters, LANES), jnp.float32)
    ranks = []
    for b in range(rows // step):
        part = onehot[:, b * step:(b + 1) * step]
        count = jnp.dot(part, earlier, preferred_element_type=jnp.float32)
        before = count[:, :step] + jnp.concatenate([carry] * (step // LANES), axis=1)
        ranks.append(jnp.sum(before * part.astype(jnp.float32), axis=0, keepdims=True))
        carry = carry + count[:, step:]
    rank = jnp.concatenate(ranks, axis=1)
    counts[...] = carry
    key = (ids - z * NY) * SLOTS + rank.astype(jnp.int32)

    def y_copy(i):
        d, first, count = MESSAGES[i]
        return pltpu.make_async_remote_copy(
            src_ref=outbox.at[d, pl.ds(first, count)],
            dst_ref=obuf.at[0, pl.ds(PLACE[d] * SLOTS + first, count)],
            send_sem=ysend,
            recv_sem=yrecv.at[i],
            device_id=(corpus_id((y + d) % NY, x, k), z),
            device_id_type=MESH,
        )

    def forward(way, first, count):
        there = pl.ds(first, count)
        target, to = (
            (lbuf.at[there], corpus_id(y, right, k)),
            (rbuf.at[there], corpus_id(y, left, left_core)),
            (obuf.at[1, there], sib),
        )[way]
        return pltpu.make_async_remote_copy(
            src_ref=obuf.at[0, there],
            dst_ref=target,
            send_sem=fsend.at[way],
            recv_sem=frecv.at[first // FIRST, way],
            device_id=(to, z),
            device_id_type=MESH,
        )

    slot_i = lax.broadcasted_iota(jnp.int32, (2 * SLOTS, 1), 0)
    rank_i = lax.broadcasted_iota(jnp.int32, (SLOTS, LANES), 0).astype(jnp.float32)
    load.wait()
    for pair in range(NY // 2):
        dists = ORDER[2 * pair:2 * pair + 2]
        tos = [(y + d) % NY for d in dists]
        wanted = slot_i % SLOTS + SLOTS * jnp.where(slot_i < SLOTS, tos[0], tos[1])
        pick = jnp.where(wanted == key, jnp.float32(1.0), jnp.float32(0.0)).astype(jnp.bfloat16)
        values = jnp.dot(pick, emb[...], preferred_element_type=jnp.float32)
        scale = lax.rsqrt(jnp.sum(values * values, axis=1, keepdims=True) + EPS)
        filled = jnp.concatenate([rank_i < counts[pl.ds(z * NY + to, 1), :] for to in tos], axis=0)
        head = jnp.where(filled, values[:, :LANES] * scale, jnp.float32(MARK))
        unit = jnp.concatenate([head, values[:, LANES:] * scale], axis=1).astype(jnp.bfloat16)
        for i, d in enumerate(dists):
            if d == 0:
                obuf[0, :SLOTS] = unit[i * SLOTS:(i + 1) * SLOTS]
            else:
                outbox[d] = unit[i * SLOTS:(i + 1) * SLOTS]
        if pair == 0:
            pl.semaphore_wait(barrier, NY - 1 + NZ - 1 + 5)
        for i, message in enumerate(MESSAGES):
            if message[0] in dists:
                y_copy(i).start()
        if pair == 0:
            for way in range(3):
                forward(way, 0, SLOTS).start()

    for i, (d, first, count) in enumerate(MESSAGES):
        y_copy(i).wait_recv()
        for way in range(3):
            forward(way, PLACE[d] * SLOTS + first, count).start()

    def col_max(s, bias):
        bias = jnp.concatenate([bias] * (s.shape[1] // LANES), axis=1)
        return jnp.max(s + bias, axis=0, keepdims=True)

    def row_max(s, bias):
        s = s + bias
        best = s[:, :LANES]
        for i in range(1, s.shape[1] // LANES):
            best = jnp.maximum(best, s[:, i * LANES:(i + 1) * LANES])
        return best

    def to_lanes(m):
        return jnp.max(m.T, axis=0, keepdims=True)

    def piece(ref, p):
        return ref[p * PIECE:(p + 1) * PIECE]

    def dot(left, right):
        return jnp.dot(left, right, preferred_element_type=jnp.float32)

    def await_part(part, way):
        forward(way, part * FIRST, UNIT - FIRST if part else FIRST).wait_recv()

    own_unit = obuf[0]
    own_rows, own_lanes = row_bias(own_unit), lane_bias(own_unit)
    for p in range(PIECES):
        own_t[:, p * PIECE:(p + 1) * PIECE] = piece(own_unit, p).T
    own_best = jnp.full((1, UNIT), NEG, jnp.float32)
    for p in range(PIECES):
        s = dot(piece(own_unit, p), own_t[...])
        same = lax.broadcasted_iota(jnp.int32, s.shape, 0) + p * PIECE == (
            lax.broadcasted_iota(jnp.int32, s.shape, 1)
        )
        best = col_max(jnp.where(same, jnp.float32(NEG), s), piece(own_rows, p))
        own_best = jnp.maximum(own_best, best)

    await_part(0, 2)
    await_part(1, 2)
    which = 1 - left // 2
    beside = obuf[which]
    beside_lanes = lane_bias(beside)
    for p in range(PIECES):
        beside_t[:, p * PIECE:(p + 1) * PIECE] = piece(beside, p).T
        sib_piece = obuf[1, p * PIECE:(p + 1) * PIECE]
        best = col_max(dot(sib_piece, own_t[...]), row_bias(sib_piece))
        own_best = jnp.maximum(own_best, best)

    beside_best = jnp.full((1, UNIT), NEG, jnp.float32)
    left_best, right_best, left_lanes, right_lanes = [], [], [], []
    for p in range(PIECES):
        there = slice(p * PIECE, (p + 1) * PIECE)
        if p * PIECE in (0, FIRST):
            await_part(p * PIECE // FIRST, 0)
            await_part(p * PIECE // FIRST, 1)
        left_piece, right_piece = lbuf[there], rbuf[there]
        left_rows, right_rows = row_bias(left_piece), row_bias(right_piece)
        left_lanes.append(lane_bias(left_piece))
        right_lanes.append(lane_bias(right_piece))
        right_t[:, there] = right_piece.T
        if p < PIECES - 1:
            left_t[:, there] = left_piece.T
        s = dot(left_piece, beside_t[...])
        beside_best = jnp.maximum(beside_best, col_max(s, left_rows))
        left_acc = row_max(s, beside_lanes)

        s = dot(right_piece, own_t[...])
        own_best = jnp.maximum(own_best, col_max(s, right_rows))
        right_acc = row_max(s, own_lanes)

        s = dot(left_piece, right_t[:, :(p + 1) * PIECE])
        left_acc = jnp.maximum(left_acc, row_max(s, jnp.concatenate(right_lanes, axis=1)))
        best = col_max(s, left_rows)
        for q in range(p):
            right_best[q] = jnp.maximum(right_best[q], best[:, q * PIECE:(q + 1) * PIECE])
        right_best.append(best[:, p * PIECE:])
        if p > 0:
            s = dot(right_piece, left_t[:, :p * PIECE])
            right_acc = jnp.maximum(right_acc, row_max(s, jnp.concatenate(left_lanes[:p], axis=1)))
            best = col_max(s, right_rows)
            for q in range(p):
                left_best[q] = jnp.maximum(left_best[q], best[:, q * PIECE:(q + 1) * PIECE])
        left_best.append(to_lanes(left_acc))
        right_best[p] = jnp.maximum(right_best[p], to_lanes(right_acc))
    left_best = jnp.concatenate(left_best, axis=1)
    right_best = jnp.concatenate(right_best, axis=1)
    beside_own = which.astype(jnp.float32)
    own_best = jnp.maximum(own_best, beside_best + beside_own * NEG)
    sib_best = beside_best + (1.0 - beside_own) * NEG

    def give(way):
        to = (corpus_id(y, left, k), corpus_id(y, right, right_core), sib)[way]
        return pltpu.make_async_remote_copy(
            src_ref=part_out.at[way],
            dst_ref=part_in.at[way],
            send_sem=psend,
            recv_sem=precv,
            device_id=(to, z),
            device_id_type=MESH,
        )

    def as_tile(v):
        pieces = [v[:, i * LANES:(i + 1) * LANES] for i in range(UNIT // LANES)]
        return jnp.concatenate(pieces + [jnp.zeros((8 - len(pieces), LANES), jnp.float32)], axis=0)

    for way, v in ((1, right_best), (0, left_best), (2, sib_best)):
        part_out[way] = as_tile(v)
        give(way).start()
    final = jnp.maximum(as_tile(own_best), -1.0)

    def whole(ref, send_sem, recv_sem):
        return pltpu.make_async_remote_copy(
            src_ref=ref, dst_ref=ref, send_sem=send_sem, recv_sem=recv_sem,
            device_id=(sib, z), device_id_type=MESH,
        )

    whole(part_in, psend, precv).wait_recv()
    for way in range(3):
        final = jnp.maximum(final, part_in[way])

    home = z * NY + y
    for d in range(NY):
        row = final[PLACE[d] // 2:PLACE[d] // 2 + 1]
        if PLACE[d] % 2:
            row = jnp.concatenate([row[:, SLOTS:], row[:, :SLOTS]], axis=1)
        ret_out[(y + NY - d) % NY] = row
        if d == 0:
            ret_in[home] = row
    for i in range(NY * NZ - 1):
        to = i + (i + NY * NZ - home) // (NY * NZ)
        pltpu.make_async_remote_copy(
            src_ref=ret_out.at[to % NY],
            dst_ref=ret_in.at[home],
            send_sem=ret_send,
            recv_sem=ret_recv,
            device_id=(corpus_id(to % NY, x, k), to // NY),
            device_id_type=MESH,
        ).start()
    returned = whole(ret_in.at[pl.ds(0, NY * NZ - 1)], ret_send, ret_recv)
    returned.wait_recv()

    table = ret_in[...].reshape(clusters, LANES)[:, :SLOTS]
    terms = []
    for _ in range(3):
        terms.append(table.astype(jnp.bfloat16))
        table = table - terms[-1].astype(jnp.float32)
    found = lax.dot_general(
        jnp.concatenate(terms, axis=0), thrice[...], (((0,), (0,)), ((), ())),
        preferred_element_type=jnp.float32,
    )
    rank_i = lax.broadcasted_iota(jnp.int32, (SLOTS, rows), 0)
    hit = rank_i == rank.astype(jnp.int32)
    out_ref[...] = jnp.sum(jnp.where(hit, found, 0.0), axis=0, keepdims=True)

    whole(outbox.at[pl.ds(1, NY - 1)], ysend, ysend).wait_send()
    for way in range(3):
        whole(obuf.at[0], fsend.at[way], fsend.at[way]).wait_send()
    whole(part_out, psend, precv).wait_send()
    returned.wait_send()


def local(embeddings, cluster_ids):
    rows, width = embeddings.shape
    dma = pltpu.SemaphoreType.DMA
    best = pl.pallas_call(
        kernel,
        out_shape=jax.ShapeDtypeStruct((1, rows), jnp.float32),
        in_specs=[pl.BlockSpec(memory_space=pltpu.HBM)] * 2,
        out_specs=pl.BlockSpec(memory_space=pltpu.VMEM),
        scratch_shapes=[
            pltpu.VMEM((rows, width), jnp.bfloat16),
            pltpu.VMEM((1, rows), jnp.int32),
            pltpu.VMEM((NY * NZ, LANES), jnp.float32),
            pltpu.VMEM((3 * NY * NZ, rows), jnp.bfloat16),
            pltpu.VMEM((NY, SLOTS, width), jnp.bfloat16),
            pltpu.VMEM((2, UNIT, width), jnp.bfloat16),
            pltpu.VMEM((UNIT, width), jnp.bfloat16),
            pltpu.VMEM((UNIT, width), jnp.bfloat16),
            *[pltpu.VMEM((width, UNIT), jnp.bfloat16)] * 4,
            pltpu.VMEM((3, 8, LANES), jnp.float32),
            pltpu.VMEM((3, 8, LANES), jnp.float32),
            pltpu.VMEM((NY, 1, LANES), jnp.float32),
            pltpu.VMEM((NY * NZ, 1, LANES), jnp.float32),
            dma, dma,
            dma, dma((len(MESSAGES),)),
            dma((3,)), dma((2, 3)),
            dma, dma, dma, dma,
        ],
        compiler_params=pltpu.CompilerParams(
            collective_id=0, has_side_effects=True, vmem_limit_bytes=55222 * 2 ** 10
        ),
        name="cluster_best",
    )(embeddings, cluster_ids.reshape(1, rows))
    return best.reshape(rows)


def solution(mesh):
    in_specs = (P("corpus", None), P("corpus"))
    out_specs = P("corpus")
    return jax.shard_map(local, mesh=mesh, in_specs=in_specs, out_specs=out_specs, check_vma=False)
```

```python
import functools

import jax
import jax.numpy as jnp
from jax import lax
from jax.experimental import pallas as pl
from jax.experimental.pallas import tpu as pltpu
from jax.sharding import PartitionSpec as P

EPS = 1e-06
MESH = pl.DeviceIdType.MESH
NY, NX, NZ = 8, 4, 8
SLOTS = 64
UNIT = NY * SLOTS
PIECE = 128
PIECES = UNIT // PIECE
FIRST = 3 * PIECE
LANES = 128
MARK = 4.0
NEG = -1e6
ORDER = (0, 1, 7, 2, 6, 3, 5, 4)
PLACE = {d: ORDER.index(d) for d in ORDER}
MESSAGES = (
    [(d, 0, 64) for d in (1, 7, 2, 6)]
    + [(d, at, 32) for at in (0, 32) for d in (3, 5)]
    + [(4, at, 16) for at in (0, 16, 32, 48)]
)


def corpus_id(y, x, k):
    return (y * NX + x) * 2 + k


def inner(left, right):
    return lax.dot_general(
        left, right, (((1,), (1,)), ((), ())), preferred_element_type=jnp.float32
    )


def row_bias(unit):
    head = unit[:, :LANES].astype(jnp.float32)
    return jnp.where(head > MARK / 2, jnp.float32(NEG), jnp.float32(0.0))


def lane_bias(unit):
    first = (lax.broadcasted_iota(jnp.int32, (16, LANES), 1) == 0).astype(jnp.bfloat16)
    head = inner(first, unit[:, :LANES])[0:1]
    return jnp.where(head > MARK / 2, jnp.float32(NEG), jnp.float32(0.0))


def kernel(
    emb_hbm, ids_hbm, out_ref,
    emb, ids_ref, counts, outbox, obuf, lbuf, rbuf, own_t, beside_t, left_t, right_t, part_out, part_in, ret_out, ret_in,
    emb_sem, ids_sem, ysend, yrecv, fsend, frecv, psend, precv,
    ret_send, ret_recv,
):
    corpus = lax.axis_index("corpus")
    z = lax.axis_index("tile")
    y, x, k = corpus // (NX * 2), (corpus // 2) % NX, corpus % 2
    right, left = (x + 1) % NX, (x + NX - 1) % NX
    right_core = (k + x // 2) % 2
    left_core = (k + left // 2) % 2
    sib = corpus_id(y, x, 1 - k)
    rows, width = emb.shape

    ids_load = pltpu.make_async_copy(ids_hbm, ids_ref, ids_sem)
    ids_load.start()
    load = pltpu.make_async_copy(emb_hbm, emb, emb_sem)
    load.start()

    barrier = pltpu.get_barrier_semaphore()

    def greet(corpus_to, tile_to):
        pl.semaphore_signal(barrier, inc=1, device_id=(corpus_to, tile_to), device_id_type=MESH)

    for d in range(1, NY):
        greet(corpus_id((y + d) % NY, x, k), z)
    for core in range(2):
        greet(corpus_id(y, right, core), z)
        greet(corpus_id(y, left, core), z)
    greet(sib, z)
    for d in range(1, NZ):
        greet(corpus, (z + d) % NZ)

    ids_load.wait()
    ids = ids_ref[...]
    clusters = NY * NZ
    member = lax.broadcasted_iota(jnp.int32, (clusters, rows), 0) == ids
    onehot = jnp.where(member, jnp.float32(1.0), jnp.float32(0.0)).astype(jnp.bfloat16)
    step = 256
    row_i = lax.broadcasted_iota(jnp.int32, (step, step + LANES), 0)
    col_i = lax.broadcasted_iota(jnp.int32, (step, step + LANES), 1)
    earlier = ((row_i < col_i) | (col_i >= step)).astype(jnp.bfloat16)
    parts = [onehot[:, b * step:(b + 1) * step] for b in range(rows // step)]
    count = jnp.dot(
        jnp.concatenate(parts, axis=0), earlier, preferred_element_type=jnp.float32
    ).reshape(len(parts), clusters, step + LANES)
    carry = jnp.zeros((clusters, LANES), jnp.float32)
    ranks = []
    for b, part in enumerate(parts):
        before = count[b, :, :step] + jnp.concatenate([carry] * (step // LANES), axis=1)
        ranks.append(jnp.sum(before * part.astype(jnp.float32), axis=0, keepdims=True))
        carry = carry + count[b, :, step:]
    rank = jnp.concatenate(ranks, axis=1)
    counts[...] = carry
    key = (ids - z * NY) * SLOTS + rank.astype(jnp.int32)

    def y_copy(i):
        d, first, count = MESSAGES[i]
        return pltpu.make_async_remote_copy(
            src_ref=outbox.at[d, pl.ds(first, count)],
            dst_ref=obuf.at[0, pl.ds(PLACE[d] * SLOTS + first, count)],
            send_sem=ysend,
            recv_sem=yrecv.at[i],
            device_id=(corpus_id((y + d) % NY, x, k), z),
            device_id_type=MESH,
        )

    def forward(way, first, count):
        there = pl.ds(first, count)
        target, to = (
            (lbuf.at[there], corpus_id(y, right, k)),
            (rbuf.at[there], corpus_id(y, left, left_core)),
            (obuf.at[1, there], sib),
        )[way]
        return pltpu.make_async_remote_copy(
            src_ref=obuf.at[0, there],
            dst_ref=target,
            send_sem=fsend.at[way],
            recv_sem=frecv.at[first // FIRST, way],
            device_id=(to, z),
            device_id_type=MESH,
        )

    slot_i = lax.broadcasted_iota(jnp.int32, (2 * SLOTS, 1), 0)
    rank_i = lax.broadcasted_iota(jnp.int32, (SLOTS, LANES), 0).astype(jnp.float32)
    load.wait()
    for pair in range(NY // 2):
        dists = ORDER[2 * pair:2 * pair + 2]
        tos = [(y + d) % NY for d in dists]
        wanted = slot_i % SLOTS + SLOTS * jnp.where(slot_i < SLOTS, tos[0], tos[1])
        pick = jnp.where(wanted == key, jnp.float32(1.0), jnp.float32(0.0)).astype(jnp.bfloat16)
        values = jnp.dot(pick, emb[...], preferred_element_type=jnp.float32)
        scale = lax.rsqrt(jnp.sum(values * values, axis=1, keepdims=True) + EPS)
        filled = jnp.concatenate([rank_i < counts[pl.ds(z * NY + to, 1), :] for to in tos], axis=0)
        head = jnp.where(filled, values[:, :LANES] * scale, jnp.float32(MARK))
        unit = jnp.concatenate([head, values[:, LANES:] * scale], axis=1).astype(jnp.bfloat16)
        for i, d in enumerate(dists):
            if d == 0:
                obuf[0, :SLOTS] = unit[i * SLOTS:(i + 1) * SLOTS]
            else:
                outbox[d] = unit[i * SLOTS:(i + 1) * SLOTS]
        if pair == 0:
            pl.semaphore_wait(barrier, NY - 1 + NZ - 1 + 5)
        for i, message in enumerate(MESSAGES):
            if message[0] in dists:
                y_copy(i).start()
        if pair == 0:
            for way in range(3):
                forward(way, 0, SLOTS).start()

    for i, (d, first, count) in enumerate(MESSAGES):
        y_copy(i).wait_recv()
        for way in range(3):
            forward(way, PLACE[d] * SLOTS + first, count).start()

    def col_max(s, bias):
        bias = jnp.concatenate([bias] * (s.shape[1] // LANES), axis=1)
        return jnp.max(s + bias, axis=0, keepdims=True)

    def row_max(s, bias):
        s = s + bias
        best = s[:, :LANES]
        for i in range(1, s.shape[1] // LANES):
            best = jnp.maximum(best, s[:, i * LANES:(i + 1) * LANES])
        return best

    def to_lanes(m):
        return jnp.max(m.T, axis=0, keepdims=True)

    def piece(ref, p):
        return ref[p * PIECE:(p + 1) * PIECE]

    def dot(left, right):
        return jnp.dot(left, right, preferred_element_type=jnp.float32)

    def await_part(part, way):
        forward(way, part * FIRST, UNIT - FIRST if part else FIRST).wait_recv()

    own_unit = obuf[0]
    own_rows, own_lanes = row_bias(own_unit), lane_bias(own_unit)
    for p in range(PIECES):
        own_t[:, p * PIECE:(p + 1) * PIECE] = piece(own_unit, p).T
    own_best = jnp.full((1, UNIT), NEG, jnp.float32)
    for p in range(PIECES):
        s = dot(piece(own_unit, p), own_t[...])
        same = lax.broadcasted_iota(jnp.int32, s.shape, 0) + p * PIECE == (
            lax.broadcasted_iota(jnp.int32, s.shape, 1)
        )
        best = col_max(jnp.where(same, jnp.float32(NEG), s), piece(own_rows, p))
        own_best = jnp.maximum(own_best, best)

    await_part(0, 2)
    await_part(1, 2)
    which = 1 - left // 2
    beside = obuf[which]
    beside_lanes = lane_bias(beside)
    for p in range(PIECES):
        beside_t[:, p * PIECE:(p + 1) * PIECE] = piece(beside, p).T
        sib_piece = obuf[1, p * PIECE:(p + 1) * PIECE]
        best = col_max(dot(sib_piece, own_t[...]), row_bias(sib_piece))
        own_best = jnp.maximum(own_best, best)

    beside_best = jnp.full((1, UNIT), NEG, jnp.float32)
    left_best, right_best, left_lanes, right_lanes = [], [], [], []
    for p in range(PIECES):
        there = slice(p * PIECE, (p + 1) * PIECE)
        if p * PIECE in (0, FIRST):
            await_part(p * PIECE // FIRST, 0)
            await_part(p * PIECE // FIRST, 1)
        left_piece, right_piece = lbuf[there], rbuf[there]
        left_rows, right_rows = row_bias(left_piece), row_bias(right_piece)
        left_lanes.append(lane_bias(left_piece))
        right_lanes.append(lane_bias(right_piece))
        right_t[:, there] = right_piece.T
        if p < PIECES - 1:
            left_t[:, there] = left_piece.T
        s = dot(left_piece, beside_t[...])
        beside_best = jnp.maximum(beside_best, col_max(s, left_rows))
        left_acc = row_max(s, beside_lanes)

        s = dot(right_piece, own_t[...])
        own_best = jnp.maximum(own_best, col_max(s, right_rows))
        right_acc = row_max(s, own_lanes)

        s = dot(left_piece, right_t[:, :(p + 1) * PIECE])
        left_acc = jnp.maximum(left_acc, row_max(s, jnp.concatenate(right_lanes, axis=1)))
        best = col_max(s, left_rows)
        for q in range(p):
            right_best[q] = jnp.maximum(right_best[q], best[:, q * PIECE:(q + 1) * PIECE])
        right_best.append(best[:, p * PIECE:])
        if p > 0:
            s = dot(right_piece, left_t[:, :p * PIECE])
            right_acc = jnp.maximum(right_acc, row_max(s, jnp.concatenate(left_lanes[:p], axis=1)))
            best = col_max(s, right_rows)
            for q in range(p):
                left_best[q] = jnp.maximum(left_best[q], best[:, q * PIECE:(q + 1) * PIECE])
        left_best.append(to_lanes(left_acc))
        right_best[p] = jnp.maximum(right_best[p], to_lanes(right_acc))
    left_best = jnp.concatenate(left_best, axis=1)
    right_best = jnp.concatenate(right_best, axis=1)
    beside_own = which.astype(jnp.float32)
    own_best = jnp.maximum(own_best, beside_best + beside_own * NEG)
    sib_best = beside_best + (1.0 - beside_own) * NEG

    def give(way):
        to = (corpus_id(y, left, k), corpus_id(y, right, right_core), sib)[way]
        return pltpu.make_async_remote_copy(
            src_ref=part_out.at[way],
            dst_ref=part_in.at[way],
            send_sem=psend,
            recv_sem=precv,
            device_id=(to, z),
            device_id_type=MESH,
        )

    def as_tile(v):
        pieces = [v[:, i * LANES:(i + 1) * LANES] for i in range(UNIT // LANES)]
        return jnp.concatenate(pieces + [jnp.zeros((8 - len(pieces), LANES), jnp.float32)], axis=0)

    for way, v in ((1, right_best), (0, left_best), (2, sib_best)):
        part_out[way] = as_tile(v)
        give(way).start()
    final = jnp.maximum(as_tile(own_best), -1.0)

    def whole(ref, send_sem, recv_sem):
        return pltpu.make_async_remote_copy(
            src_ref=ref, dst_ref=ref, send_sem=send_sem, recv_sem=recv_sem,
            device_id=(sib, z), device_id_type=MESH,
        )

    whole(part_in, psend, precv).wait_recv()
    for way in range(3):
        final = jnp.maximum(final, part_in[way])

    home = z * NY + y
    for d in range(NY):
        row = final[PLACE[d] // 2:PLACE[d] // 2 + 1]
        if PLACE[d] % 2:
            row = jnp.concatenate([row[:, SLOTS:], row[:, :SLOTS]], axis=1)
        ret_out[(y + NY - d) % NY] = row
        if d == 0:
            ret_in[home] = row
    for i in range(NY * NZ - 1):
        to = i + (i + NY * NZ - home) // (NY * NZ)
        pltpu.make_async_remote_copy(
            src_ref=ret_out.at[to % NY],
            dst_ref=ret_in.at[home],
            send_sem=ret_send,
            recv_sem=ret_recv,
            device_id=(corpus_id(to % NY, x, k), to // NY),
            device_id_type=MESH,
        ).start()
    returned = whole(ret_in.at[pl.ds(0, NY * NZ - 1)], ret_send, ret_recv)
    returned.wait_recv()

    table = ret_in[...].reshape(clusters, LANES)[:, :SLOTS]
    found = jnp.zeros((SLOTS, rows), jnp.float32)
    for _ in range(3):
        rounded = table.astype(jnp.bfloat16)
        table = table - rounded.astype(jnp.float32)
        found = found + lax.dot_general(
            rounded, onehot, (((0,), (0,)), ((), ())), preferred_element_type=jnp.float32
        )
    rank_i = lax.broadcasted_iota(jnp.int32, (SLOTS, rows), 0)
    hit = rank_i == rank.astype(jnp.int32)
    out_ref[...] = jnp.sum(jnp.where(hit, found, 0.0), axis=0, keepdims=True)

    whole(outbox.at[pl.ds(1, NY - 1)], ysend, ysend).wait_send()
    for way in range(3):
        whole(obuf.at[0], fsend.at[way], fsend.at[way]).wait_send()
    whole(part_out, psend, precv).wait_send()
    returned.wait_send()


def local(embeddings, cluster_ids):
    rows, width = embeddings.shape
    dma = pltpu.SemaphoreType.DMA
    best = pl.pallas_call(
        kernel,
        out_shape=jax.ShapeDtypeStruct((1, rows), jnp.float32),
        in_specs=[pl.BlockSpec(memory_space=pltpu.HBM)] * 2,
        out_specs=pl.BlockSpec(memory_space=pltpu.VMEM),
        scratch_shapes=[
            pltpu.VMEM((rows, width), jnp.bfloat16),
            pltpu.VMEM((1, rows), jnp.int32),
            pltpu.VMEM((NY * NZ, LANES), jnp.float32),
            pltpu.VMEM((NY, SLOTS, width), jnp.bfloat16),
            pltpu.VMEM((2, UNIT, width), jnp.bfloat16),
            pltpu.VMEM((UNIT, width), jnp.bfloat16),
            pltpu.VMEM((UNIT, width), jnp.bfloat16),
            *[pltpu.VMEM((width, UNIT), jnp.bfloat16)] * 4,
            pltpu.VMEM((3, 8, LANES), jnp.float32),
            pltpu.VMEM((3, 8, LANES), jnp.float32),
            pltpu.VMEM((NY, 1, LANES), jnp.float32),
            pltpu.VMEM((NY * NZ, 1, LANES), jnp.float32),
            dma, dma,
            dma, dma((len(MESSAGES),)),
            dma((3,)), dma((2, 3)),
            dma, dma, dma, dma,
        ],
        compiler_params=pltpu.CompilerParams(
            collective_id=0, has_side_effects=True, vmem_limit_bytes=55222 * 2 ** 10
        ),
        name="cluster_best",
    )(embeddings, cluster_ids.reshape(1, rows))
    return best.reshape(rows)


def solution(mesh):
    in_specs = (P("corpus", None), P("corpus"))
    out_specs = P("corpus")
    return jax.shard_map(local, mesh=mesh, in_specs=in_specs, out_specs=out_specs, check_vma=False)
```
